32 devices in a mesh: group: 2 (over y), tensor: 4 (over z), batch: 4 (over x, core).
Axes of the slice: x: 2, y: 2, z: 4, core: 2. Of those that a mesh axis runs over, the one named last changes fastest.
Arguments:
- hidden_input: bfloat16 [2, 512, 8192], P(None, ('group', 'batch'), 'tensor'), parts along dimension 1, may hold values from -6 to 6
- projection_weight: bfloat16 [8192, 8192], P('tensor', 'batch'), may hold values from -0.0625 to 0.0625
- adapter_down_rows: bfloat16 [128, 64, 8192], P('batch', None, 'tensor'), may hold values from -0.0625 to 0.0625
- adapter_up_rows: bfloat16 [128, 64, 8192], P('batch', None, 'tensor'), may hold values from -0.75 to 0.75
- adapter_row_map: int32 [256], P('group'), parts along dimension 0, may hold values from 0 to 127, as said below
- segment_index_rows: int32 [2, 8, 64], P(None, ('group', 'batch')), parts along dimension 1, may hold values from 0 to 3, never falling along the last dimension, each value on 1 to 32 neighbouring positions
- segment_adapter: int32 [2, 8, 4], P(None, 'group'), parts along dimension 1, may hold values from 0 to 127, as said below
Outputs:
- projected: bfloat16 [2, 512, 8192], P(None, ('group', 'batch'), 'tensor'), parts along dimension 1
The draws below stay inside these ranges and needn't reach their ends.
There are 2 independent parts, one for each index of `group`. The reference program is written for one: setup_inputs(seed, part) draws one part's arguments, and reference() takes and returns one part's arrays. A program takes and returns all parts, laid end to end along the dimension named above; an argument that names none is the same for every part. Nothing has to cross between parts.
Inputs may be any that keep to these rules, and one draw needn't show every extreme that they name: A permutation: adapter a's factors are row adapter_row_map[a] of adapter_down_rows and adapter_up_rows, stored on index adapter_row_map[a] // 32 of batch. `segment_adapter`: within one step and one index of batch the 4 entries are different adapters; of them exactly 0 or 2 are stored on each index of batch, so at most 2 and this most is reached. `segment_index_rows`: never falling along a device's requests; every segment has at least one request.
All inputs are finite; a program needn't handle non-finite values.
Results may differ from the reference program's by a relative error of at most 0.012.
Values may be sent and summed in bfloat16 or wider, within the bound.
A program may use at most 192 MiB of HBM per device.

```python
import math
import jax
import jax.numpy as jnp
import numpy as np
from jax import lax

MODEL_WIDTH = 8192
OUTPUT_FEATURES = 8192
ADAPTER_RANK = 64
STEPS = 2
SEGMENT_SLOTS = 4
CAP = 2
REQ_DEV = 64
ADP_DEV = 32
REQUESTS = 256
ADAPTER_TOTAL = 128
N_TENSOR = 4
N_BATCH = 4


def storage_rows(key):
    return jax.random.permutation(key, ADAPTER_TOTAL).astype(jnp.int32)


def draw_adapter_row_map(key, part):
    return storage_rows(key)


def draw_segment_adapter(key, part):
    permuted = storage_rows(key)
    inverse = jnp.argsort(permuted).astype(jnp.int32)
    key = jax.random.fold_in(key, 5)
    first_key, second_key, third_key = jax.random.split(key, 3)
    groups = SEGMENT_SLOTS // CAP
    offset = jax.random.randint(first_key, (STEPS, N_BATCH, 1), 0, N_BATCH)
    owner_dev = (offset + jnp.arange(groups, dtype=jnp.int32)[None, None, :]) % N_BATCH
    scores = jax.random.randint(second_key, (STEPS, N_BATCH, groups, ADP_DEV), 0, 1 << 20) * ADP_DEV
    scores = scores + jnp.arange(ADP_DEV, dtype=jnp.int32)
    chosen = jnp.argsort(scores, axis=-1)[..., :CAP].astype(jnp.int32)
    position = (owner_dev[..., None] * ADP_DEV + chosen).reshape(STEPS, N_BATCH, SEGMENT_SLOTS)
    order_scores = jax.random.randint(third_key, (STEPS, N_BATCH, SEGMENT_SLOTS), 0, 1 << 20) * SEGMENT_SLOTS
    order_scores = order_scores + jnp.arange(SEGMENT_SLOTS, dtype=jnp.int32)
    order = jnp.argsort(order_scores, axis=-1).astype(jnp.int32)
    position = jnp.take_along_axis(position, order, axis=-1)
    return inverse[position]


def levels(stream_key, dims, cuts, low, high):
    factor_of = 1.0
    for dim, blocks in cuts:
        heights = jax.random.uniform(jax.random.fold_in(jax.random.fold_in(stream_key, 6), dim), (blocks,), jnp.float32, low / len(cuts), high / len(cuts))
        factor_of = factor_of * jnp.repeat(jnp.exp(heights), dims[dim] // blocks).reshape((-1,) + (1,) * (len(dims) - 1 - dim))
    return factor_of


def split_up(count, total, bound, skew):
    portions = [(1 << 20) // math.isqrt(grade ** skew) + 1 for grade in range(2, count + 1)]
    rest, holding = total - bound - (count - 1), [1] * (count - 1)
    while rest > 0:
        candidates = [i for i in range(count - 1) if holding[i] < bound]
        whole, budget = sum([portions[i] for i in candidates]), rest
        for i in candidates:
            extra = min(bound - holding[i], max(1, budget * portions[i] // whole), rest)
            holding[i] = holding[i] + extra
            rest = rest - extra
    return np.array([bound] + holding)


def ragged(key, number_of, total, bound, skew):
    if number_of == 2:
        one = jax.random.randint(key, (), max(1, total - bound), min(bound, total - 1) + 1)
        return jnp.stack([one, total - one])
    tallies = jnp.asarray(split_up(number_of, total, bound, skew), jnp.int32)
    pairs = (number_of - 1) // 2
    donor, taker = tallies[1:1 + 2 * pairs:2], tallies[2:2 + 2 * pairs:2]
    slack = jnp.minimum(donor - 1, bound - taker)
    shifted = jax.random.randint(jax.random.fold_in(key, 1), (pairs,), 0, 1 << 20) % (slack + 1)
    tallies = tallies.at[1:1 + 2 * pairs:2].set(donor - shifted).at[2:2 + 2 * pairs:2].set(taker + shifted)
    return tallies[jax.random.permutation(jax.random.fold_in(key, 2), number_of)]


def gaussian(rng, shape, scale, bound, cuts=(), kind=jnp.bfloat16):
    array = scale * jax.random.normal(rng, shape, jnp.float32)
    if cuts:
        array = array * levels(rng, shape, cuts, -0.22, 0.18)
    return jnp.clip(array, -bound, bound).astype(kind)


def setup_inputs(seed: int = 0, part: int = 0) -> dict:
    arg_keys = jax.random.split(jax.random.key(seed), 8)
    own_keys = jax.random.split(jax.random.fold_in(arg_keys[7], part), 8)
    return {
        "hidden_input": gaussian(own_keys[0], (STEPS, REQUESTS, MODEL_WIDTH), 1.0, 6.0, ((1, 4), (2, 4))),
        "projection_weight": gaussian(arg_keys[1], (MODEL_WIDTH, OUTPUT_FEATURES), MODEL_WIDTH ** -0.5, 0.0625, ((0, 4), (1, 4))),
        "adapter_down_rows": gaussian(arg_keys[2], (ADAPTER_TOTAL, ADAPTER_RANK, MODEL_WIDTH), MODEL_WIDTH ** -0.5, 0.0625, ((0, 4), (2, 4))),
        "adapter_up_rows": gaussian(arg_keys[3], (ADAPTER_TOTAL, ADAPTER_RANK, OUTPUT_FEATURES), ADAPTER_RANK ** -0.5, 0.75, ((0, 4), (2, 4))),
        "adapter_row_map": draw_adapter_row_map(jax.random.fold_in(jax.random.fold_in(arg_keys[7], part), 71), part),
        "segment_index_rows": jax.vmap(lambda own: jnp.searchsorted(jnp.cumsum(ragged(own, SEGMENT_SLOTS, REQ_DEV, REQ_DEV // 2, 2)), jnp.arange(REQ_DEV), side="right"))(jax.random.split(own_keys[5], STEPS * N_BATCH)).reshape((STEPS, N_BATCH, REQ_DEV)).astype(jnp.int32),
        "segment_adapter": draw_segment_adapter(jax.random.fold_in(jax.random.fold_in(arg_keys[7], part), 71), part),
    }


def round_half(values):
    rounded = values.astype(jnp.bfloat16)
    rounded = lax.optimization_barrier(rounded)
    return rounded.astype(jnp.float32)


def reference(hidden_input, projection_weight, adapter_down_rows, adapter_up_rows, adapter_row_map, segment_index_rows, segment_adapter):
    stored = adapter_row_map[segment_adapter]
    block_span_width = MODEL_WIDTH // N_TENSOR
    weight_blocks = projection_weight.reshape(N_TENSOR, block_span_width, OUTPUT_FEATURES)
    results = []
    for step_index in range(STEPS):
        inputs = hidden_input[step_index]
        input_blocks = jnp.transpose(inputs.reshape(REQUESTS, N_TENSOR, block_span_width), (1, 0, 2))

        def add_block(total, block):
            rows, weights = block
            piece = jnp.dot(rows, weights, preferred_element_type=jnp.float32)
            return total + round_half(piece), None

        base, _ = lax.scan(add_block, jnp.zeros((REQUESTS, OUTPUT_FEATURES), jnp.float32), (input_blocks, weight_blocks))

        def one_block(block):
            block_rows, segment_row, stored_block = block
            down_factor_slots = adapter_down_rows[stored_block].astype(jnp.float32).reshape(SEGMENT_SLOTS, ADAPTER_RANK, N_TENSOR, block_span_width)
            up_factor_slots = adapter_up_rows[stored_block]
            rows_split = block_rows.astype(jnp.float32).reshape(REQ_DEV, N_TENSOR, block_span_width)
            shrink_all = jnp.einsum("rtd,jktd->trjk", rows_split, down_factor_slots,
                                    precision=lax.Precision.HIGHEST)
            onehot = (segment_row[:, None] == jnp.arange(SEGMENT_SLOTS, dtype=jnp.int32)[None, :]).astype(jnp.float32)
            pieces = jnp.sum(onehot[None, :, :, None] * shrink_all, axis=2)
            shrink = jnp.sum(round_half(pieces), axis=0).astype(jnp.bfloat16)
            masked = (onehot.astype(jnp.bfloat16)[:, :, None] * shrink[:, None, :]).reshape(REQ_DEV, SEGMENT_SLOTS * ADAPTER_RANK)
            return jnp.dot(masked, up_factor_slots.reshape(SEGMENT_SLOTS * ADAPTER_RANK, OUTPUT_FEATURES), preferred_element_type=jnp.float32)

        adapter_term = lax.map(one_block, (inputs.reshape(N_BATCH, REQ_DEV, MODEL_WIDTH), segment_index_rows[step_index],
                                           stored[step_index]))
        results.append((base + adapter_term.reshape(REQUESTS, OUTPUT_FEATURES)).astype(jnp.bfloat16))
    return jnp.stack(results)
```

```python
import jax
import jax.numpy as jnp
from jax import lax
from jax.sharding import PartitionSpec as P

CAP = 2


def owned_slots(segment_adapter, adapter_row_map, stored_count, own_index):
    slot_count = segment_adapter.shape[-1]
    position = jnp.take(adapter_row_map, segment_adapter, axis=0)
    owned = position // stored_count == own_index
    local_index = position % stored_count
    rank = jnp.cumsum(owned.astype(jnp.int32), axis=-1) - 1
    picked = owned[..., None, :] & (rank[..., None, :] == jnp.arange(CAP)[:, None])
    slot = jnp.sum(jnp.where(picked, jnp.arange(slot_count), 0), axis=-1)
    local = jnp.sum(jnp.where(picked, local_index[..., None, :], 0), axis=-1)
    filled = jnp.any(picked, axis=-1)
    return slot, local, filled


def shards_general(
    hidden_input,
    projection_weight,
    adapter_down_rows,
    adapter_up_rows,
    adapter_row_map,
    segment_index_rows,
    segment_adapter,
):
    steps, req, _ = hidden_input.shape
    batch_count = lax.axis_size("batch")
    stored_count, rank_width, _ = adapter_down_rows.shape
    own_index = lax.axis_index("batch")
    hidden = lax.all_gather(hidden_input, "batch", axis=1, tiled=True)
    segments = lax.all_gather(segment_index_rows, "batch", axis=1, tiled=True)
    slot, local, filled = owned_slots(segment_adapter, adapter_row_map, stored_count, own_index)
    mask = (segments[..., None] == slot[:, :, None, :]) & filled[:, :, None, :]
    grouped = hidden.reshape(steps, batch_count, req, -1)
    down = jnp.take(adapter_down_rows, local, axis=0)
    shrink_all = jnp.einsum("sbrd,sbckd->sbrck", grouped, down, preferred_element_type=jnp.float32)
    shrink_part = jnp.sum(jnp.where(mask[..., None], shrink_all, 0.0), axis=3)
    shrink = lax.psum(shrink_part.astype(jnp.bfloat16), "tensor")
    base_part = jnp.einsum(
        "srd,do->sro", hidden, projection_weight, preferred_element_type=jnp.float32
    ).astype(jnp.bfloat16)
    base_rows = lax.all_to_all(base_part, "batch", split_axis=1, concat_axis=2, tiled=True)
    base = lax.psum_scatter(base_rows, "tensor", scatter_dimension=2, tiled=True)
    masked = jnp.where(mask[..., None], shrink[:, :, :, None, :], jnp.zeros((), jnp.bfloat16))
    masked = masked.reshape(steps, batch_count, req, CAP * rank_width)
    up = jnp.take(adapter_up_rows, local, axis=0)
    up = up.reshape(steps, batch_count, CAP * rank_width, -1)
    term = jnp.einsum("sbrm,sbmo->sbro", masked, up, preferred_element_type=jnp.float32)
    term = lax.psum_scatter(term.astype(jnp.bfloat16), "batch", scatter_dimension=1, tiled=False)
    return (base.astype(jnp.float32) + term.astype(jnp.float32)).astype(jnp.bfloat16)


def solution(mesh):
    in_specs = (
        P(None, ("group", "batch"), "tensor"),
        P("tensor", "batch"),
        P("batch", None, "tensor"),
        P("batch", None, "tensor"),
        P("group"),
        P(None, ("group", "batch"), None),
        P(None, "group", None),
    )
    out_specs = P(None, ("group", "batch"), "tensor")
    return jax.shard_map(
        shards_general, mesh=mesh, in_specs=in_specs, out_specs=out_specs, check_vma=False
    )
```

```python
import jax
import jax.numpy as jnp
from jax import lax
from jax.experimental import pallas as pl
from jax.experimental.pallas import tpu as pltpu
from jax.sharding import PartitionSpec as P

CAP = 2
SIDE = 4
MESH = pl.DeviceIdType.MESH


def owned_slots(segment_adapter, adapter_row_map, stored_count, own_index):
    slot_count = segment_adapter.shape[-1]
    position = jnp.take(adapter_row_map, segment_adapter, axis=0)
    owned = position // stored_count == own_index
    local_index = position % stored_count
    rank = jnp.cumsum(owned.astype(jnp.int32), axis=-1) - 1
    picked = owned[..., None, :] & (rank[..., None, :] == jnp.arange(CAP)[:, None])
    slot = jnp.sum(jnp.where(picked, jnp.arange(slot_count), 0), axis=-1)
    local = jnp.sum(jnp.where(picked, local_index[..., None, :], 0), axis=-1)
    filled = jnp.any(picked, axis=-1)
    return slot, local, filled


def shards_general(
    hidden_input,
    projection_weight,
    adapter_down_rows,
    adapter_up_rows,
    adapter_row_map,
    segment_index_rows,
    segment_adapter,
):
    steps, req, _ = hidden_input.shape
    batch_count = lax.axis_size("batch")
    stored_count, rank_width, _ = adapter_down_rows.shape
    own_index = lax.axis_index("batch")
    hidden = lax.all_gather(hidden_input, "batch", axis=1, tiled=True)
    segments = lax.all_gather(segment_index_rows, "batch", axis=1, tiled=True)
    slot, local, filled = owned_slots(segment_adapter, adapter_row_map, stored_count, own_index)
    mask = (segments[..., None] == slot[:, :, None, :]) & filled[:, :, None, :]
    grouped = hidden.reshape(steps, batch_count, req, -1)
    down = jnp.take(adapter_down_rows, local, axis=0)
    shrink_all = jnp.einsum("sbrd,sbckd->sbrck", grouped, down, preferred_element_type=jnp.float32)
    shrink_part = jnp.sum(jnp.where(mask[..., None], shrink_all, 0.0), axis=3)
    shrink = lax.psum(shrink_part.astype(jnp.bfloat16), "tensor")
    base_part = jnp.einsum(
        "srd,do->sro", hidden, projection_weight, preferred_element_type=jnp.float32
    ).astype(jnp.bfloat16)
    base_rows = lax.all_to_all(base_part, "batch", split_axis=1, concat_axis=2, tiled=True)
    base = lax.psum_scatter(base_rows, "tensor", scatter_dimension=2, tiled=True)
    masked = jnp.where(mask[..., None], shrink[:, :, :, None, :], jnp.zeros((), jnp.bfloat16))
    masked = masked.reshape(steps, batch_count, req, CAP * rank_width)
    up = jnp.take(adapter_up_rows, local, axis=0)
    up = up.reshape(steps, batch_count, CAP * rank_width, -1)
    term = jnp.einsum("sbrm,sbmo->sbro", masked, up, preferred_element_type=jnp.float32)
    term = lax.psum_scatter(term.astype(jnp.bfloat16), "batch", scatter_dimension=1, tiled=False)
    return (base.astype(jnp.float32) + term.astype(jnp.float32)).astype(jnp.bfloat16)


def fused_kernel(
    table_ref,
    map_ref,
    seg_ref,
    hid_ref,
    w_ref,
    down_ref,
    up_ref,
    out_ref,
    hid,
    w_v,
    down_v,
    up_v,
    seg_v,
    pieces,
    rows,
    z_down,
    z_up,
    sh_own,
    sh_recv,
    term,
    pass_in,
    mine_in,
    far_in,
    acc,
    load_sem,
    seg_send,
    seg_recv,
    hid_send,
    hid_recv,
    row_send,
    row_recv,
    z_send,
    zd_recv,
    zu_recv,
    sh_send,
    sh_recv_sem,
    term_send,
    term_recv,
):
    steps, req, width = hid_ref.shape
    stored, rank, out_width = up_ref.shape
    columns = w_ref.shape[1]
    t = lax.axis_index("tensor")
    b = lax.axis_index("batch")
    twin = b + 1 - 2 * (b % 2)
    across = (b + 2) % SIDE
    far = 3 - b
    order = (b, twin, across, far)

    def remote(src, dst, send, recv, **where):
        return pltpu.make_async_remote_copy(
            src_ref=src,
            dst_ref=dst,
            send_sem=send,
            recv_sem=recv,
            device_id=where,
            device_id_type=MESH,
        )

    own_load = [
        pltpu.make_async_copy(hid_ref.at[s], hid.at[s, b], load_sem.at[3 + s])
        for s in range(steps)
    ]
    w_load = pltpu.make_async_copy(w_ref, w_v, load_sem.at[0])
    down_load = pltpu.make_async_copy(down_ref, down_v, load_sem.at[1])
    up_load = pltpu.make_async_copy(up_ref, up_v, load_sem.at[2])
    for copy in own_load:
        copy.start()
    w_load.start()
    down_load.start()
    up_load.start()
    seg_v[b] = jnp.zeros(seg_v.shape[1:], jnp.int32)
    for s in range(steps):
        seg_v[b, s : s + 1, 0:req] = seg_ref[s]

    barrier = pltpu.get_barrier_semaphore()
    for k in range(1, SIDE):
        pl.semaphore_signal(
            barrier, inc=1, device_id={"batch": (b + k) % SIDE}, device_id_type=MESH
        )
        pl.semaphore_signal(
            barrier, inc=1, device_id={"tensor": (t + k) % SIDE}, device_id_type=MESH
        )
    pl.semaphore_wait(barrier, 2 * (SIDE - 1))

    sent = []

    def go(copy):
        copy.start()
        sent.append(copy)

    def hid_copy(s, kind, src, index, to):
        return remote(
            src, hid.at[s, index], hid_send.at[s, kind], hid_recv.at[s, index], batch=to
        )

    for s in range(steps):
        go(hid_copy(s, 0, hid_ref.at[s], b, across))
    for s in range(steps):
        go(hid_copy(s, 1, hid_ref.at[s], b, twin))
    for k in range(1, SIDE):
        go(remote(seg_v.at[b], seg_v.at[b], seg_send.at[k], seg_recv.at[b], batch=order[k]))

    def slots(s, other):
        first_slot, first_row = jnp.int32(-1), jnp.int32(0)
        last_slot, last_row = jnp.int32(-1), jnp.int32(0)
        for j in range(table_ref.shape[2]):
            position = map_ref[table_ref[s, other, j]]
            held = position // stored == b
            row = position % stored
            first = held & (first_slot < 0)
            last_slot = jnp.where(held, j, last_slot)
            last_row = jnp.where(held, row, last_row)
            first_row = jnp.where(first, row, first_row)
            first_slot = jnp.where(first, j, first_slot)
        return first_slot, first_row, last_slot, last_row

    tile = min(512, columns)

    def base(s):
        @pl.loop(0, columns // tile)
        def _(i):
            span = pl.ds(pl.multiple_of(i * tile, tile), tile)
            value = jnp.dot(
                hid[s].reshape(SIDE * req, width),
                w_v[:, span],
                preferred_element_type=jnp.float32,
            )
            pieces[s, :, :, span] = value.astype(jnp.bfloat16).reshape(SIDE, req, tile)

    def shrink(s):
        @pl.loop(0, SIDE)
        def _(other):
            first_slot, first_row, last_slot, last_row = slots(s, other)
            factors = jnp.concatenate([down_v[first_row], down_v[last_row]], axis=0)
            value = lax.dot_general(
                hid[s, other],
                factors,
                (((1,), (1,)), ((), ())),
                preferred_element_type=jnp.float32,
            )
            line = seg_v[other, s : s + 1, 0:req].astype(jnp.float32)
            diagonal = lax.broadcasted_iota(
                jnp.int32, (req, req), 0
            ) == lax.broadcasted_iota(jnp.int32, (req, req), 1)
            segment = jnp.sum(
                jnp.where(diagonal, jnp.broadcast_to(line, (req, req)), 0.0),
                axis=1,
                keepdims=True,
            )
            lane = lax.broadcasted_iota(jnp.int32, (req, CAP * rank), 1)
            wanted = jnp.where(lane < rank, first_slot, last_slot).astype(jnp.float32)
            sh_own[s, other] = jnp.where(segment == wanted, value, 0.0).astype(jnp.bfloat16)

        for k in range(1, SIDE):
            to = (t + k) % SIDE
            go(
                remote(
                    sh_own.at[s],
                    sh_recv.at[s, k - 1],
                    sh_send.at[s, k - 1],
                    sh_recv_sem.at[s, k - 1],
                    tensor=to,
                )
            )

    def row_copy(s, k, index):
        return remote(
            pieces.at[s, order[k]],
            rows.at[s, index],
            row_send.at[s, k],
            row_recv.at[s, index],
            batch=order[k],
        )

    for s in range(steps):
        hid_copy(s, 0, hid_ref.at[s], across, across).wait_recv()
        go(hid_copy(s, 2, hid.at[s, across], across, twin))
        own_load[s].wait()
        hid_copy(s, 1, hid_ref.at[s], twin, twin).wait_recv()
        hid_copy(s, 2, hid.at[s, far], far, twin).wait_recv()
        if s == 0:
            w_load.wait()
        base(s)
        for k in (2, 3, 1):
            go(row_copy(s, k, b))
        rows[s, b] = pieces[s, b]
        if s == 0:
            down_load.wait()
            for k in range(1, SIDE):
                remote(
                    seg_v.at[b], seg_v.at[order[k]], seg_send.at[k], seg_recv.at[order[k]],
                    batch=order[k],
                ).wait_recv()
        shrink(s)

    term_tile = min(512, out_width)

    def term_copy(s, kind, src, dst, to):
        return remote(src, dst, term_send.at[s, kind], term_recv.at[s, kind], batch=to)

    def terms(s):
        for k in range(SIDE - 1):
            remote(
                sh_own.at[s],
                sh_recv.at[s, k],
                sh_send.at[s, k],
                sh_recv_sem.at[s, k],
                tensor=(t + 1) % SIDE,
            ).wait_recv()
        if s == 0:
            up_load.wait()

        @pl.loop(0, SIDE)
        def _(other):
            _, first_row, _, last_row = slots(s, other)
            total = sh_own[s, other].astype(jnp.float32)
            for k in range(SIDE - 1):
                total = total + sh_recv[s, k, other].astype(jnp.float32)
            masked = total.astype(jnp.bfloat16)
            for i in range(out_width // term_tile):
                span = pl.ds(i * term_tile, term_tile)
                factors = jnp.concatenate(
                    [up_v[first_row, :, span], up_v[last_row, :, span]], axis=0
                )
                term[s, other, :, span] = jnp.dot(
                    masked, factors, preferred_element_type=jnp.float32
                ).astype(jnp.bfloat16)

        go(term_copy(s, 0, term.at[s, far], pass_in.at[s], twin))
        go(term_copy(s, 1, term.at[s, twin], mine_in.at[s], twin))

    def terms_across(s):
        term_copy(s, 0, term.at[s, far], pass_in.at[s], twin).wait_recv()
        term[s, across] = term[s, across] + pass_in[s]
        go(term_copy(s, 2, term.at[s, across], far_in.at[s], across))

    def z_copy(s, c, up):
        return remote(
            rows.at[s, c],
            (z_up if up else z_down).at[s, c],
            z_send.at[s, c],
            (zu_recv if up else zd_recv).at[s, c],
            tensor=(t + 1) % SIDE if up else (t + SIDE - 1) % SIDE,
        )

    def z_item(s, k):
        c = order[k]
        if k:
            row_copy(s, k, c).wait_recv()
        for up in (False, True):
            moves = t < c if up else t > c
            inner = t > 0 if up else t < SIDE - 1

            @pl.when(moves & inner)
            def _():
                remote(
                    rows.at[s, c],
                    (z_up if up else z_down).at[s, c],
                    z_send.at[s, c],
                    (zu_recv if up else zd_recv).at[s, c],
                    tensor=(t + 1) % SIDE,
                ).wait_recv()
                got = (z_up if up else z_down)[s, c].astype(jnp.float32)
                rows[s, c] = (rows[s, c].astype(jnp.float32) + got).astype(jnp.bfloat16)

            @pl.when(moves)
            def _():
                z_copy(s, c, up).start()

    z_item(0, 0)
    z_item(0, 1)
    terms(0)
    z_item(1, 0)
    z_item(1, 1)
    z_item(0, 2)
    z_item(0, 3)
    terms(1)
    terms_across(0)
    z_item(1, 2)
    z_item(1, 3)
    terms_across(1)

    for s in range(steps):
        term_copy(s, 1, term.at[s, twin], mine_in.at[s], twin).wait_recv()
        acc[...] = (
            rows[s, t].astype(jnp.float32)
            + term[s, b].astype(jnp.float32)
            + mine_in[s].astype(jnp.float32)
        )
        for up in (False, True):

            @pl.when(t > 0 if up else t < SIDE - 1)
            def _():
                remote(
                    rows.at[s, t],
                    (z_up if up else z_down).at[s, t],
                    z_send.at[s, t],
                    (zu_recv if up else zd_recv).at[s, t],
                    tensor=(t + 1) % SIDE,
                ).wait_recv()
                acc[...] += (z_up if up else z_down)[s, t].astype(jnp.float32)

        term_copy(s, 2, term.at[s, across], far_in.at[s], across).wait_recv()
        out_ref[s] = (acc[...] + far_in[s].astype(jnp.float32)).astype(jnp.bfloat16)

    for copy in sent:
        copy.wait_send()
    for s in range(steps):
        for c in range(SIDE):

            @pl.when(t != c)
            def _():
                z_copy(s, c, True).wait_send()


def shards_fused(
    hidden_input,
    projection_weight,
    adapter_down_rows,
    adapter_up_rows,
    adapter_row_map,
    segment_index_rows,
    segment_adapter,
):
    steps, req, width = hidden_input.shape
    columns = projection_weight.shape[1]
    stored, rank, out_width = adapter_up_rows.shape
    bf16 = jnp.bfloat16
    dma = pltpu.SemaphoreType.DMA
    vmem = pl.BlockSpec(memory_space=pltpu.VMEM)
    smem = pl.BlockSpec(memory_space=pltpu.SMEM)
    whole = pl.BlockSpec(memory_space=pl.ANY)
    block = (steps, SIDE, req, out_width)
    scratch = [
        pltpu.VMEM((steps, SIDE, req, width), bf16),
        pltpu.VMEM(projection_weight.shape, bf16),
        pltpu.VMEM(adapter_down_rows.shape, bf16),
        pltpu.VMEM(adapter_up_rows.shape, bf16),
        pltpu.VMEM((SIDE, 8, 128), jnp.int32),
        pltpu.VMEM((steps, SIDE, req, columns), bf16),
        pltpu.VMEM(block, bf16),
        pltpu.VMEM(block, bf16),
        pltpu.VMEM(block, bf16),
        pltpu.VMEM((steps, SIDE, req, CAP * rank), bf16),
        pltpu.VMEM((steps, SIDE - 1, SIDE, req, CAP * rank), bf16),
        pltpu.VMEM(block, bf16),
        pltpu.VMEM((steps, req, out_width), bf16),
        pltpu.VMEM((steps, req, out_width), bf16),
        pltpu.VMEM((steps, req, out_width), bf16),
        pltpu.VMEM((req, out_width), jnp.float32),
        dma((3 + steps,)),
        dma((SIDE,)),
        dma((SIDE,)),
        dma((steps, 3)),
        dma((steps, SIDE)),
        dma((steps, SIDE)),
        dma((steps, SIDE)),
        dma((steps, SIDE)),
        dma((steps, SIDE)),
        dma((steps, SIDE)),
        dma((steps, SIDE)),
        dma((steps, SIDE)),
        dma((steps, 3)),
        dma((steps, 3)),
    ]
    return pl.pallas_call(
        fused_kernel,
        out_shape=jax.ShapeDtypeStruct((steps, req, out_width), bf16),
        in_specs=[smem, smem, vmem, whole, whole, whole, whole],
        out_specs=vmem,
        scratch_shapes=scratch,
        compiler_params=pltpu.CompilerParams(
            collective_id=0, has_side_effects=True, vmem_limit_bytes=56 * 1024 * 1024
        ),
        name="fused_projection",
    )(
        segment_adapter,
        adapter_row_map,
        segment_index_rows,
        hidden_input,
        projection_weight,
        adapter_down_rows,
        adapter_up_rows,
    )


def solution(mesh):
    in_specs = (
        P(None, ("group", "batch"), "tensor"),
        P("tensor", "batch"),
        P("batch", None, "tensor"),
        P("batch", None, "tensor"),
        P("group"),
        P(None, ("group", "batch"), None),
        P(None, "group", None),
    )
    out_specs = P(None, ("group", "batch"), "tensor")
    fused = mesh.shape["tensor"] == SIDE and mesh.shape["batch"] == SIDE
    return jax.shard_map(
        shards_fused if fused else shards_general, mesh=mesh, in_specs=in_specs, out_specs=out_specs, check_vma=False
    )
```

```python
import jax
import jax.numpy as jnp
from jax import lax
from jax.experimental import pallas as pl
from jax.experimental.pallas import tpu as pltpu
from jax.sharding import PartitionSpec as P

CAP = 2
SIDE = 4
PARTS = 4
MESH = pl.DeviceIdType.MESH


def owned_slots(segment_adapter, adapter_row_map, stored_count, own_index):
    slot_count = segment_adapter.shape[-1]
    position = jnp.take(adapter_row_map, segment_adapter, axis=0)
    owned = position // stored_count == own_index
    local_index = position % stored_count
    rank = jnp.cumsum(owned.astype(jnp.int32), axis=-1) - 1
    picked = owned[..., None, :] & (rank[..., None, :] == jnp.arange(CAP)[:, None])
    slot = jnp.sum(jnp.where(picked, jnp.arange(slot_count), 0), axis=-1)
    local = jnp.sum(jnp.where(picked, local_index[..., None, :], 0), axis=-1)
    filled = jnp.any(picked, axis=-1)
    return slot, local, filled


def shards_general(
    hidden_input,
    projection_weight,
    adapter_down_rows,
    adapter_up_rows,
    adapter_row_map,
    segment_index_rows,
    segment_adapter,
):
    steps, req, _ = hidden_input.shape
    batch_count = lax.axis_size("batch")
    stored_count, rank_width, _ = adapter_down_rows.shape
    own_index = lax.axis_index("batch")
    hidden = lax.all_gather(hidden_input, "batch", axis=1, tiled=True)
    segments = lax.all_gather(segment_index_rows, "batch", axis=1, tiled=True)
    slot, local, filled = owned_slots(segment_adapter, adapter_row_map, stored_count, own_index)
    mask = (segments[..., None] == slot[:, :, None, :]) & filled[:, :, None, :]
    grouped = hidden.reshape(steps, batch_count, req, -1)
    down = jnp.take(adapter_down_rows, local, axis=0)
    shrink_all = jnp.einsum("sbrd,sbckd->sbrck", grouped, down, preferred_element_type=jnp.float32)
    shrink_part = jnp.sum(jnp.where(mask[..., None], shrink_all, 0.0), axis=3)
    shrink = lax.psum(shrink_part.astype(jnp.bfloat16), "tensor")
    base_part = jnp.einsum(
        "srd,do->sro", hidden, projection_weight, preferred_element_type=jnp.float32
    ).astype(jnp.bfloat16)
    base_rows = lax.all_to_all(base_part, "batch", split_axis=1, concat_axis=2, tiled=True)
    base = lax.psum_scatter(base_rows, "tensor", scatter_dimension=2, tiled=True)
    masked = jnp.where(mask[..., None], shrink[:, :, :, None, :], jnp.zeros((), jnp.bfloat16))
    masked = masked.reshape(steps, batch_count, req, CAP * rank_width)
    up = jnp.take(adapter_up_rows, local, axis=0)
    up = up.reshape(steps, batch_count, CAP * rank_width, -1)
    term = jnp.einsum("sbrm,sbmo->sbro", masked, up, preferred_element_type=jnp.float32)
    term = lax.psum_scatter(term.astype(jnp.bfloat16), "batch", scatter_dimension=1, tiled=False)
    return (base.astype(jnp.float32) + term.astype(jnp.float32)).astype(jnp.bfloat16)


def fused_kernel(
    table_ref,
    map_ref,
    seg_ref,
    hid_ref,
    w_ref,
    down_ref,
    up_ref,
    out_ref,
    hid,
    w_v,
    down_v,
    up_v,
    seg_v,
    pieces,
    rows,
    z_down,
    z_up,
    sh_own,
    sh_recv,
    term,
    pass_in,
    mine_in,
    far_in,
    acc,
    load_sem,
    seg_send,
    seg_recv,
    hid_send,
    hid_recv,
    row_send,
    row_recv,
    z_send,
    zd_recv,
    zu_recv,
    sh_send,
    sh_recv_sem,
    term_send,
    term_recv,
):
    steps, req, width = hid_ref.shape
    stored, rank, out_width = up_ref.shape
    columns = w_ref.shape[1]
    t = lax.axis_index("tensor")
    b = lax.axis_index("batch")
    twin = b + 1 - 2 * (b % 2)
    across = (b + 2) % SIDE
    far = 3 - b
    order = (b, twin, across, far)

    def remote(src, dst, send, recv, **where):
        return pltpu.make_async_remote_copy(
            src_ref=src,
            dst_ref=dst,
            send_sem=send,
            recv_sem=recv,
            device_id=where,
            device_id_type=MESH,
        )

    own_load = [
        pltpu.make_async_copy(hid_ref.at[s], hid.at[b, s], load_sem.at[3 + s])
        for s in range(steps)
    ]
    w_load = pltpu.make_async_copy(w_ref, w_v, load_sem.at[0])
    down_load = pltpu.make_async_copy(down_ref, down_v, load_sem.at[1])
    up_load = pltpu.make_async_copy(up_ref, up_v, load_sem.at[2])
    for copy in own_load:
        copy.start()
    w_load.start()
    seg_v[b] = jnp.zeros(seg_v.shape[1:], jnp.int32)
    for s in range(steps):
        seg_v[b, s : s + 1, 0:req] = seg_ref[s]

    barrier = pltpu.get_barrier_semaphore()
    for k in range(1, SIDE):
        pl.semaphore_signal(
            barrier, inc=1, device_id={"batch": (b + k) % SIDE}, device_id_type=MESH
        )
        pl.semaphore_signal(
            barrier, inc=1, device_id={"tensor": (t + k) % SIDE}, device_id_type=MESH
        )
    pl.semaphore_wait(barrier, 2 * (SIDE - 1))

    sent = []

    def go(copy):
        copy.start()
        sent.append(copy)

    def hid_copy(s, kind, src, index, to):
        return remote(
            src, hid.at[index, s], hid_send.at[s, kind], hid_recv.at[s, index], batch=to
        )

    for s in range(steps):
        go(hid_copy(s, 0, hid_ref.at[s], b, across))
    for s in range(steps):
        go(hid_copy(s, 1, hid_ref.at[s], b, twin))
    for k in range(1, SIDE):
        go(remote(seg_v.at[b], seg_v.at[b], seg_send.at[k], seg_recv.at[b], batch=order[k]))

    def slots(s, other):
        first_slot, first_row = jnp.int32(-1), jnp.int32(0)
        last_slot, last_row = jnp.int32(-1), jnp.int32(0)
        for j in range(table_ref.shape[2]):
            position = map_ref[table_ref[s, other, j]]
            held = position // stored == b
            row = position % stored
            first = held & (first_slot < 0)
            last_slot = jnp.where(held, j, last_slot)
            last_row = jnp.where(held, row, last_row)
            first_row = jnp.where(first, row, first_row)
            first_slot = jnp.where(first, j, first_slot)
        return first_slot, first_row, last_slot, last_row

    tile = min(512, columns)
    near_pair = 2 * (b // 2)
    far_pair = (near_pair + 2) % SIDE

    def base_near():
        @pl.loop(0, columns // tile)
        def _(i):
            span = pl.ds(pl.multiple_of(i * tile, tile), tile)
            value = jnp.dot(
                hid[pl.ds(near_pair, 2)].reshape(2 * steps * req, width),
                w_v[:, span],
                preferred_element_type=jnp.float32,
            ).astype(jnp.bfloat16)
            pieces[pl.ds(near_pair, 2), :, :, span] = value.reshape(2, steps, req, tile)

    def base_far(s):
        @pl.loop(0, columns // tile)
        def _(i):
            span = pl.ds(pl.multiple_of(i * tile, tile), tile)
            value = jnp.dot(
                hid[pl.ds(far_pair, 2), s].reshape(2 * req, width),
                w_v[:, span],
                preferred_element_type=jnp.float32,
            ).astype(jnp.bfloat16)
            pieces[pl.ds(far_pair, 2), s, :, span] = value.reshape(2, req, tile)

    def shrink(s):
        @pl.loop(0, SIDE)
        def _(other):
            first_slot, first_row, last_slot, last_row = slots(s, other)
            factors = jnp.concatenate([down_v[first_row], down_v[last_row]], axis=0)
            value = lax.dot_general(
                hid[other, s],
                factors,
                (((1,), (1,)), ((), ())),
                preferred_element_type=jnp.float32,
            )
            line = seg_v[other, s : s + 1, 0:req].astype(jnp.float32)
            diagonal = lax.broadcasted_iota(
                jnp.int32, (req, req), 0
            ) == lax.broadcasted_iota(jnp.int32, (req, req), 1)
            segment = jnp.sum(
                jnp.where(diagonal, jnp.broadcast_to(line, (req, req)), 0.0),
                axis=1,
                keepdims=True,
            )
            lane = lax.broadcasted_iota(jnp.int32, (req, CAP * rank), 1)
            wanted = jnp.where(lane < rank, first_slot, last_slot).astype(jnp.float32)
            sh_own[s, other] = jnp.where(segment == wanted, value, 0.0).astype(jnp.bfloat16)

        for k in range(1, SIDE):
            to = (t + k) % SIDE
            go(
                remote(
                    sh_own.at[s],
                    sh_recv.at[s, k - 1],
                    sh_send.at[s, k - 1],
                    sh_recv_sem.at[s, k - 1],
                    tensor=to,
                )
            )

    half = req // PARTS

    def row_copy(s, k, h, index):
        part = pl.ds(h * half, half)
        return remote(
            pieces.at[order[k], s, part],
            rows.at[s, index, part],
            row_send.at[s, k, h],
            row_recv.at[s, index, h],
            batch=order[k],
        )

    def z_part(s, c, h, up):
        part = pl.ds(h * half, half)
        return remote(
            rows.at[s, c, part],
            (z_up if up else z_down).at[s, c, part],
            z_send.at[s, c, h],
            (zu_recv if up else zd_recv).at[s, c, h],
            tensor=(t + 1) % SIDE if up else (t + SIDE - 1) % SIDE,
        )

    def z_begin(s, k):
        c = order[k]
        for h in range(PARTS):
            if k:
                row_copy(s, k, h, c).wait_recv()
            for up in (False, True):

                @pl.when((t == 0) & (c > 0) if up else (t == SIDE - 1) & (c < SIDE - 1))
                def _():
                    z_part(s, c, h, up).start()

    def z_relay(s, k):
        c = order[k]
        for h in range(PARTS):
            part = pl.ds(h * half, half)
            for up in (False, True):
                inner = (t > 0) & (t < c) if up else (t < SIDE - 1) & (t > c)

                @pl.when(inner)
                def _():
                    z_part(s, c, h, up).wait_recv()
                    got = (z_up if up else z_down)[s, c, part].astype(jnp.float32)
                    total = rows[s, c, part].astype(jnp.float32) + got
                    rows[s, c, part] = total.astype(jnp.bfloat16)
                    z_part(s, c, h, up).start()

    term_tile = min(512, out_width)

    def term_copy(s, kind, src, dst, to):
        return remote(src, dst, term_send.at[s, kind], term_recv.at[s, kind], batch=to)

    def terms(s):
        for k in range(SIDE - 1):
            remote(
                sh_own.at[s],
                sh_recv.at[s, k],
                sh_send.at[s, k],
                sh_recv_sem.at[s, k],
                tensor=(t + 1) % SIDE,
            ).wait_recv()
        if s == 0:
            up_load.wait()

        @pl.loop(0, SIDE)
        def _(other):
            _, first_row, _, last_row = slots(s, other)
            total = sh_own[s, other].astype(jnp.float32)
            for k in range(SIDE - 1):
                total = total + sh_recv[s, k, other].astype(jnp.float32)
            masked = total.astype(jnp.bfloat16)
            for i in range(out_width // term_tile):
                span = pl.ds(i * term_tile, term_tile)
                factors = jnp.concatenate(
                    [up_v[first_row, :, span], up_v[last_row, :, span]], axis=0
                )
                term[s, other, :, span] = jnp.dot(
                    masked, factors, preferred_element_type=jnp.float32
                ).astype(jnp.bfloat16)

        go(term_copy(s, 0, term.at[s, far], pass_in.at[s], twin))
        go(term_copy(s, 1, term.at[s, twin], mine_in.at[s], twin))

    def terms_across(s):
        term_copy(s, 0, term.at[s, far], pass_in.at[s], twin).wait_recv()
        term[s, across] = term[s, across] + pass_in[s]
        go(term_copy(s, 2, term.at[s, across], far_in.at[s], across))

    for s in range(steps):
        own_load[s].wait()
        hid_copy(s, 1, hid_ref.at[s], twin, twin).wait_recv()
    w_load.wait()
    down_load.start()
    up_load.start()
    base_near()
    for s in range(steps):
        for h in range(PARTS):
            go(row_copy(s, 1, h, b))
        rows[s, b] = pieces[b, s]
    z_begin(0, 0)

    def far_half(s):
        hid_copy(s, 0, hid_ref.at[s], across, across).wait_recv()
        go(hid_copy(s, 2, hid.at[across, s], across, twin))
        hid_copy(s, 2, hid.at[far, s], far, twin).wait_recv()
        base_far(s)
        for k in (2, 3):
            for h in range(PARTS):
                go(row_copy(s, k, h, b))

    far_half(0)
    down_load.wait()
    for k in range(1, SIDE):
        remote(
            seg_v.at[b], seg_v.at[order[k]], seg_send.at[k], seg_recv.at[order[k]], batch=order[k]
        ).wait_recv()
    shrink(0)
    z_begin(0, 1)
    far_half(1)
    shrink(1)
    z_begin(1, 0)
    z_begin(1, 1)
    z_relay(0, 0)
    z_begin(0, 2)
    terms(0)
    z_relay(0, 1)
    terms_across(0)
    terms(1)
    z_relay(0, 2)
    z_begin(0, 3)
    terms_across(1)
    z_relay(1, 0)
    z_relay(0, 3)
    z_begin(1, 2)
    z_relay(1, 1)
    z_begin(1, 3)
    z_relay(1, 2)
    z_relay(1, 3)

    for s in range(steps):
        term_copy(s, 1, term.at[s, twin], mine_in.at[s], twin).wait_recv()
        acc[...] = (
            rows[s, t].astype(jnp.float32)
            + term[s, b].astype(jnp.float32)
            + mine_in[s].astype(jnp.float32)
        )
        for up in (False, True):

            @pl.when(t > 0 if up else t < SIDE - 1)
            def _():
                for h in range(PARTS):
                    z_part(s, t, h, up).wait_recv()
                acc[...] += (z_up if up else z_down)[s, t].astype(jnp.float32)

        term_copy(s, 2, term.at[s, across], far_in.at[s], across).wait_recv()
        out_ref[s] = (acc[...] + far_in[s].astype(jnp.float32)).astype(jnp.bfloat16)

    for copy in sent:
        copy.wait_send()
    for s in range(steps):
        for c in range(SIDE):
            for h in range(PARTS):

                @pl.when(t != c)
                def _():
                    z_part(s, c, h, True).wait_send()


def shards_fused(
    hidden_input,
    projection_weight,
    adapter_down_rows,
    adapter_up_rows,
    adapter_row_map,
    segment_index_rows,
    segment_adapter,
):
    steps, req, width = hidden_input.shape
    columns = projection_weight.shape[1]
    stored, rank, out_width = adapter_up_rows.shape
    bf16 = jnp.bfloat16
    dma = pltpu.SemaphoreType.DMA
    vmem = pl.BlockSpec(memory_space=pltpu.VMEM)
    smem = pl.BlockSpec(memory_space=pltpu.SMEM)
    whole = pl.BlockSpec(memory_space=pl.ANY)
    block = (steps, SIDE, req, out_width)
    scratch = [
        pltpu.VMEM((SIDE, steps, req, width), bf16),
        pltpu.VMEM(projection_weight.shape, bf16),
        pltpu.VMEM(adapter_down_rows.shape, bf16),
        pltpu.VMEM(adapter_up_rows.shape, bf16),
        pltpu.VMEM((SIDE, 8, 128), jnp.int32),
        pltpu.VMEM((SIDE, steps, req, columns), bf16),
        pltpu.VMEM(block, bf16),
        pltpu.VMEM(block, bf16),
        pltpu.VMEM(block, bf16),
        pltpu.VMEM((steps, SIDE, req, CAP * rank), bf16),
        pltpu.VMEM((steps, SIDE - 1, SIDE, req, CAP * rank), bf16),
        pltpu.VMEM(block, bf16),
        pltpu.VMEM((steps, req, out_width), bf16),
        pltpu.VMEM((steps, req, out_width), bf16),
        pltpu.VMEM((steps, req, out_width), bf16),
        pltpu.VMEM((req, out_width), jnp.float32),
        dma((3 + steps,)),
        dma((SIDE,)),
        dma((SIDE,)),
        dma((steps, 3)),
        dma((steps, SIDE)),
        dma((steps, SIDE, PARTS)),
        dma((steps, SIDE, PARTS)),
        dma((steps, SIDE, PARTS)),
        dma((steps, SIDE, PARTS)),
        dma((steps, SIDE, PARTS)),
        dma((steps, SIDE)),
        dma((steps, SIDE)),
        dma((steps, 3)),
        dma((steps, 3)),
    ]
    return pl.pallas_call(
        fused_kernel,
        out_shape=jax.ShapeDtypeStruct((steps, req, out_width), bf16),
        in_specs=[smem, smem, vmem, whole, whole, whole, whole],
        out_specs=vmem,
        scratch_shapes=scratch,
        compiler_params=pltpu.CompilerParams(
            collective_id=0, has_side_effects=True, vmem_limit_bytes=56 * 1024 * 1024
        ),
        name="fused_projection",
    )(
        segment_adapter,
        adapter_row_map,
        segment_index_rows,
        hidden_input,
        projection_weight,
        adapter_down_rows,
        adapter_up_rows,
    )


def solution(mesh):
    in_specs = (
        P(None, ("group", "batch"), "tensor"),
        P("tensor", "batch"),
        P("batch", None, "tensor"),
        P("batch", None, "tensor"),
        P("group"),
        P(None, ("group", "batch"), None),
        P(None, "group", None),
    )
    out_specs = P(None, ("group", "batch"), "tensor")
    fused = mesh.shape["tensor"] == SIDE and mesh.shape["batch"] == SIDE
    return jax.shard_map(
        shards_fused if fused else shards_general, mesh=mesh, in_specs=in_specs, out_specs=out_specs, check_vma=False
    )
```

```python
import jax
import jax.numpy as jnp
from jax import lax
from jax.experimental import pallas as pl
from jax.experimental.pallas import tpu as pltpu
from jax.sharding import PartitionSpec as P

CAP = 2
SIDE = 4
PARTS = 2
MESH = pl.DeviceIdType.MESH


def owned_slots(segment_adapter, adapter_row_map, stored_count, own_index):
    slot_count = segment_adapter.shape[-1]
    position = jnp.take(adapter_row_map, segment_adapter, axis=0)
    owned = position // stored_count == own_index
    local_index = position % stored_count
    rank = jnp.cumsum(owned.astype(jnp.int32), axis=-1) - 1
    picked = owned[..., None, :] & (rank[..., None, :] == jnp.arange(CAP)[:, None])
    slot = jnp.sum(jnp.where(picked, jnp.arange(slot_count), 0), axis=-1)
    local = jnp.sum(jnp.where(picked, local_index[..., None, :], 0), axis=-1)
    filled = jnp.any(picked, axis=-1)
    return slot, local, filled


def shards_general(
    hidden_input,
    projection_weight,
    adapter_down_rows,
    adapter_up_rows,
    adapter_row_map,
    segment_index_rows,
    segment_adapter,
):
    steps, req, _ = hidden_input.shape
    batch_count = lax.axis_size("batch")
    stored_count, rank_width, _ = adapter_down_rows.shape
    own_index = lax.axis_index("batch")
    hidden = lax.all_gather(hidden_input, "batch", axis=1, tiled=True)
    segments = lax.all_gather(segment_index_rows, "batch", axis=1, tiled=True)
    slot, local, filled = owned_slots(segment_adapter, adapter_row_map, stored_count, own_index)
    mask = (segments[..., None] == slot[:, :, None, :]) & filled[:, :, None, :]
    grouped = hidden.reshape(steps, batch_count, req, -1)
    down = jnp.take(adapter_down_rows, local, axis=0)
    shrink_all = jnp.einsum("sbrd,sbckd->sbrck", grouped, down, preferred_element_type=jnp.float32)
    shrink_part = jnp.sum(jnp.where(mask[..., None], shrink_all, 0.0), axis=3)
    shrink = lax.psum(shrink_part.astype(jnp.bfloat16), "tensor")
    base_part = jnp.einsum(
        "srd,do->sro", hidden, projection_weight, preferred_element_type=jnp.float32
    ).astype(jnp.bfloat16)
    base_rows = lax.all_to_all(base_part, "batch", split_axis=1, concat_axis=2, tiled=True)
    base = lax.psum_scatter(base_rows, "tensor", scatter_dimension=2, tiled=True)
    masked = jnp.where(mask[..., None], shrink[:, :, :, None, :], jnp.zeros((), jnp.bfloat16))
    masked = masked.reshape(steps, batch_count, req, CAP * rank_width)
    up = jnp.take(adapter_up_rows, local, axis=0)
    up = up.reshape(steps, batch_count, CAP * rank_width, -1)
    term = jnp.einsum("sbrm,sbmo->sbro", masked, up, preferred_element_type=jnp.float32)
    term = lax.psum_scatter(term.astype(jnp.bfloat16), "batch", scatter_dimension=1, tiled=False)
    return (base.astype(jnp.float32) + term.astype(jnp.float32)).astype(jnp.bfloat16)


def fused_kernel(
    table_ref,
    map_ref,
    seg_ref,
    hid_ref,
    w_ref,
    down_ref,
    up_ref,
    out_ref,
    hid,
    w_v,
    down_v,
    up_v,
    seg_v,
    pieces,
    rows,
    z_down,
    z_up,
    sh_own,
    sh_recv,
    term,
    pass_in,
    mine_in,
    far_in,
    acc,
    load_sem,
    seg_send,
    seg_recv,
    hid_send,
    hid_recv,
    row_send,
    row_recv,
    z_send,
    zd_recv,
    zu_recv,
    sh_send,
    sh_recv_sem,
    term_send,
    term_recv,
):
    steps, req, width = hid_ref.shape
    stored, rank, out_width = up_ref.shape
    columns = w_ref.shape[1]
    t = lax.axis_index("tensor")
    b = lax.axis_index("batch")
    twin = b + 1 - 2 * (b % 2)
    across = (b + 2) % SIDE
    far = 3 - b
    order = (b, twin, across, far)

    def remote(src, dst, send, recv, **where):
        return pltpu.make_async_remote_copy(
            src_ref=src,
            dst_ref=dst,
            send_sem=send,
            recv_sem=recv,
            device_id=where,
            device_id_type=MESH,
        )

    own_load = [
        pltpu.make_async_copy(hid_ref.at[s], hid.at[b, s], load_sem.at[3 + s])
        for s in range(steps)
    ]
    w_load = pltpu.make_async_copy(w_ref, w_v, load_sem.at[0])
    down_load = pltpu.make_async_copy(down_ref, down_v, load_sem.at[1])
    up_load = pltpu.make_async_copy(up_ref, up_v, load_sem.at[2])
    for copy in own_load:
        copy.start()
    w_load.start()
    seg_v[b] = jnp.zeros(seg_v.shape[1:], jnp.int32)
    for s in range(steps):
        seg_v[b, s : s + 1, 0:req] = seg_ref[s]

    barrier = pltpu.get_barrier_semaphore()
    for k in range(1, SIDE):
        pl.semaphore_signal(
            barrier, inc=1, device_id={"batch": (b + k) % SIDE}, device_id_type=MESH
        )
        pl.semaphore_signal(
            barrier, inc=1, device_id={"tensor": (t + k) % SIDE}, device_id_type=MESH
        )
    pl.semaphore_wait(barrier, 2 * (SIDE - 1))

    sent = []

    def go(copy):
        copy.start()
        sent.append(copy)

    def hid_copy(s, kind, src, index, to):
        return remote(
            src, hid.at[index, s], hid_send.at[s, kind], hid_recv.at[s, index], batch=to
        )

    for s in range(steps):
        go(hid_copy(s, 0, hid_ref.at[s], b, across))
    for s in range(steps):
        go(hid_copy(s, 1, hid_ref.at[s], b, twin))
    for k in range(1, SIDE):
        go(remote(seg_v.at[b], seg_v.at[b], seg_send.at[k], seg_recv.at[b], batch=order[k]))

    def slots(s, other):
        first_slot, first_row = jnp.int32(-1), jnp.int32(0)
        last_slot, last_row = jnp.int32(-1), jnp.int32(0)
        for j in range(table_ref.shape[2]):
            position = map_ref[table_ref[s, other, j]]
            held = position // stored == b
            row = position % stored
            first = held & (first_slot < 0)
            last_slot = jnp.where(held, j, last_slot)
            last_row = jnp.where(held, row, last_row)
            first_row = jnp.where(first, row, first_row)
            first_slot = jnp.where(first, j, first_slot)
        return first_slot, first_row, last_slot, last_row

    tile = min(512, columns)
    near_pair = 2 * (b // 2)
    far_pair = (near_pair + 2) % SIDE

    def base_near():
        @pl.loop(0, columns // tile)
        def _(i):
            span = pl.ds(pl.multiple_of(i * tile, tile), tile)
            value = jnp.dot(
                hid[pl.ds(near_pair, 2)].reshape(2 * steps * req, width),
                w_v[:, span],
                preferred_element_type=jnp.float32,
            ).astype(jnp.bfloat16)
            pieces[pl.ds(near_pair, 2), :, :, span] = value.reshape(2, steps, req, tile)

    def base_far(s):
        @pl.loop(0, columns // tile)
        def _(i):
            span = pl.ds(pl.multiple_of(i * tile, tile), tile)
            value = jnp.dot(
                hid[pl.ds(far_pair, 2), s].reshape(2 * req, width),
                w_v[:, span],
                preferred_element_type=jnp.float32,
            ).astype(jnp.bfloat16)
            pieces[pl.ds(far_pair, 2), s, :, span] = value.reshape(2, req, tile)

    def shrink(s):
        @pl.loop(0, SIDE)
        def _(other):
            first_slot, first_row, last_slot, last_row = slots(s, other)
            factors = jnp.concatenate([down_v[first_row], down_v[last_row]], axis=0)
            value = lax.dot_general(
                hid[other, s],
                factors,
                (((1,), (1,)), ((), ())),
                preferred_element_type=jnp.float32,
            )
            line = seg_v[other, s : s + 1, 0:req].astype(jnp.float32)
            diagonal = lax.broadcasted_iota(
                jnp.int32, (req, req), 0
            ) == lax.broadcasted_iota(jnp.int32, (req, req), 1)
            segment = jnp.sum(
                jnp.where(diagonal, jnp.broadcast_to(line, (req, req)), 0.0),
                axis=1,
                keepdims=True,
            )
            lane = lax.broadcasted_iota(jnp.int32, (req, CAP * rank), 1)
            wanted = jnp.where(lane < rank, first_slot, last_slot).astype(jnp.float32)
            sh_own[s, other] = jnp.where(segment == wanted, value, 0.0).astype(jnp.bfloat16)

        for k in range(1, SIDE):
            to = (t + k) % SIDE
            go(
                remote(
                    sh_own.at[s],
                    sh_recv.at[s, k - 1],
                    sh_send.at[s, k - 1],
                    sh_recv_sem.at[s, k - 1],
                    tensor=to,
                )
            )

    half = req // PARTS

    def row_copy(s, k, h, index):
        part = pl.ds(h * half, half)
        return remote(
            pieces.at[order[k], s, part],
            rows.at[s, index, part],
            row_send.at[s, k, h],
            row_recv.at[s, index, h],
            batch=order[k],
        )

    def z_part(s, c, h, up):
        part = pl.ds(h * half, half)
        return remote(
            rows.at[s, c, part],
            (z_up if up else z_down).at[s, c, part],
            z_send.at[s, c, h],
            (zu_recv if up else zd_recv).at[s, c, h],
            tensor=(t + 1) % SIDE if up else (t + SIDE - 1) % SIDE,
        )

    def z_begin(s, k):
        c = order[k]
        for h in range(PARTS):
            if k:
                row_copy(s, k, h, c).wait_recv()
            for up in (False, True):

                @pl.when((t == 0) & (c > 0) if up else (t == SIDE - 1) & (c < SIDE - 1))
                def _():
                    z_part(s, c, h, up).start()

    def z_relay(s, k):
        c = order[k]
        for h in range(PARTS):
            part = pl.ds(h * half, half)
            for up in (False, True):
                inner = (t > 0) & (t < c) if up else (t < SIDE - 1) & (t > c)

                @pl.when(inner)
                def _():
                    z_part(s, c, h, up).wait_recv()
                    got = (z_up if up else z_down)[s, c, part].astype(jnp.float32)
                    total = rows[s, c, part].astype(jnp.float32) + got
                    rows[s, c, part] = total.astype(jnp.bfloat16)
                    z_part(s, c, h, up).start()

    term_tile = min(512, out_width)

    def term_copy(s, kind, src, dst, to):
        return remote(src, dst, term_send.at[s, kind], term_recv.at[s, kind], batch=to)

    def terms(s):
        for k in range(SIDE - 1):
            remote(
                sh_own.at[s],
                sh_recv.at[s, k],
                sh_send.at[s, k],
                sh_recv_sem.at[s, k],
                tensor=(t + 1) % SIDE,
            ).wait_recv()
        if s == 0:
            up_load.wait()

        @pl.loop(0, SIDE)
        def _(other):
            _, first_row, _, last_row = slots(s, other)
            total = sh_own[s, other].astype(jnp.float32)
            for k in range(SIDE - 1):
                total = total + sh_recv[s, k, other].astype(jnp.float32)
            masked = total.astype(jnp.bfloat16)
            for i in range(out_width // term_tile):
                span = pl.ds(i * term_tile, term_tile)
                factors = jnp.concatenate(
                    [up_v[first_row, :, span], up_v[last_row, :, span]], axis=0
                )
                term[s, other, :, span] = jnp.dot(
                    masked, factors, preferred_element_type=jnp.float32
                ).astype(jnp.bfloat16)

        go(term_copy(s, 0, term.at[s, far], pass_in.at[s], twin))
        go(term_copy(s, 1, term.at[s, twin], mine_in.at[s], twin))

    def terms_across(s):
        term_copy(s, 0, term.at[s, far], pass_in.at[s], twin).wait_recv()
        term[s, across] = term[s, across] + pass_in[s]
        go(term_copy(s, 2, term.at[s, across], far_in.at[s], across))

    for s in range(steps):
        own_load[s].wait()
        hid_copy(s, 1, hid_ref.at[s], twin, twin).wait_recv()
    w_load.wait()
    down_load.start()
    up_load.start()
    base_near()
    for s in range(steps):
        for h in range(PARTS):
            go(row_copy(s, 1, h, b))
        rows[s, b] = pieces[b, s]
    z_begin(0, 0)

    def far_half(s):
        hid_copy(s, 0, hid_ref.at[s], across, across).wait_recv()
        go(hid_copy(s, 2, hid.at[across, s], across, twin))
        hid_copy(s, 2, hid.at[far, s], far, twin).wait_recv()
        base_far(s)
        for k in (2, 3):
            for h in range(PARTS):
                go(row_copy(s, k, h, b))

    far_half(0)
    down_load.wait()
    for k in range(1, SIDE):
        remote(
            seg_v.at[b], seg_v.at[order[k]], seg_send.at[k], seg_recv.at[order[k]], batch=order[k]
        ).wait_recv()
    shrink(0)
    z_begin(0, 1)
    far_half(1)
    shrink(1)
    z_begin(1, 0)
    z_begin(1, 1)
    z_relay(0, 0)
    z_begin(0, 2)
    terms(0)
    z_relay(0, 1)
    terms_across(0)
    terms(1)
    z_relay(0, 2)
    z_begin(0, 3)
    terms_across(1)
    z_relay(1, 0)
    z_relay(0, 3)
    z_begin(1, 2)
    z_relay(1, 1)
    z_begin(1, 3)
    z_relay(1, 2)
    z_relay(1, 3)

    for s in range(steps):
        term_copy(s, 1, term.at[s, twin], mine_in.at[s], twin).wait_recv()
        acc[...] = (
            rows[s, t].astype(jnp.float32)
            + term[s, b].astype(jnp.float32)
            + mine_in[s].astype(jnp.float32)
        )
        for up in (False, True):

            @pl.when(t > 0 if up else t < SIDE - 1)
            def _():
                for h in range(PARTS):
                    z_part(s, t, h, up).wait_recv()
                acc[...] += (z_up if up else z_down)[s, t].astype(jnp.float32)

        term_copy(s, 2, term.at[s, across], far_in.at[s], across).wait_recv()
        out_ref[s] = (acc[...] + far_in[s].astype(jnp.float32)).astype(jnp.bfloat16)

    for copy in sent:
        copy.wait_send()
    for s in range(steps):
        for c in range(SIDE):
            for h in range(PARTS):

                @pl.when(t != c)
                def _():
                    z_part(s, c, h, True).wait_send()


def shards_fused(
    hidden_input,
    projection_weight,
    adapter_down_rows,
    adapter_up_rows,
    adapter_row_map,
    segment_index_rows,
    segment_adapter,
):
    steps, req, width = hidden_input.shape
    columns = projection_weight.shape[1]
    stored, rank, out_width = adapter_up_rows.shape
    bf16 = jnp.bfloat16
    dma = pltpu.SemaphoreType.DMA
    vmem = pl.BlockSpec(memory_space=pltpu.VMEM)
    smem = pl.BlockSpec(memory_space=pltpu.SMEM)
    whole = pl.BlockSpec(memory_space=pl.ANY)
    block = (steps, SIDE, req, out_width)
    scratch = [
        pltpu.VMEM((SIDE, steps, req, width), bf16),
        pltpu.VMEM(projection_weight.shape, bf16),
        pltpu.VMEM(adapter_down_rows.shape, bf16),
        pltpu.VMEM(adapter_up_rows.shape, bf16),
        pltpu.VMEM((SIDE, 8, 128), jnp.int32),
        pltpu.VMEM((SIDE, steps, req, columns), bf16),
        pltpu.VMEM(block, bf16),
        pltpu.VMEM(block, bf16),
        pltpu.VMEM(block, bf16),
        pltpu.VMEM((steps, SIDE, req, CAP * rank), bf16),
        pltpu.VMEM((steps, SIDE - 1, SIDE, req, CAP * rank), bf16),
        pltpu.VMEM(block, bf16),
        pltpu.VMEM((steps, req, out_width), bf16),
        pltpu.VMEM((steps, req, out_width), bf16),
        pltpu.VMEM((steps, req, out_width), bf16),
        pltpu.VMEM((req, out_width), jnp.float32),
        dma((3 + steps,)),
        dma((SIDE,)),
        dma((SIDE,)),
        dma((steps, 3)),
        dma((steps, SIDE)),
        dma((steps, SIDE, PARTS)),
        dma((steps, SIDE, PARTS)),
        dma((steps, SIDE, PARTS)),
        dma((steps, SIDE, PARTS)),
        dma((steps, SIDE, PARTS)),
        dma((steps, SIDE)),
        dma((steps, SIDE)),
        dma((steps, 3)),
        dma((steps, 3)),
    ]
    return pl.pallas_call(
        fused_kernel,
        out_shape=jax.ShapeDtypeStruct((steps, req, out_width), bf16),
        in_specs=[smem, smem, vmem, whole, whole, whole, whole],
        out_specs=vmem,
        scratch_shapes=scratch,
        compiler_params=pltpu.CompilerParams(
            collective_id=0, has_side_effects=True, vmem_limit_bytes=56 * 1024 * 1024
        ),
        name="fused_projection",
    )(
        segment_adapter,
        adapter_row_map,
        segment_index_rows,
        hidden_input,
        projection_weight,
        adapter_down_rows,
        adapter_up_rows,
    )


def solution(mesh):
    in_specs = (
        P(None, ("group", "batch"), "tensor"),
        P("tensor", "batch"),
        P("batch", None, "tensor"),
        P("batch", None, "tensor"),
        P("group"),
        P(None, ("group", "batch"), None),
        P(None, "group", None),
    )
    out_specs = P(None, ("group", "batch"), "tensor")
    fused = mesh.shape["tensor"] == SIDE and mesh.shape["batch"] == SIDE
    return jax.shard_map(
        shards_fused if fused else shards_general, mesh=mesh, in_specs=in_specs, out_specs=out_specs, check_vma=False
    )
```
